32 devices in a mesh: groups: 2 (over x), wide: 8 (over z, y), tp: 2 (over core).
Axes of the slice: x: 2, y: 2, z: 4, core: 2. Of those that a mesh axis runs over, the one named last changes fastest.
Arguments:
- hidden: bfloat16 [16, 2, 5120], P(('groups', 'wide')), parts along dimension 0, may hold values from -6 to 6
- kv_weight: bfloat16 [5120, 2048], P('tp'), may hold values from -0.078125 to 0.078125
- adapter_down: float32 [2, 2560, 128], P('tp', 'wide'), may hold values from -0.078125 to 0.078125
- adapter_up: float32 [64, 2048], P(None, ('wide', 'tp')), may hold values from -0.375 to 0.375
- key_gain: float32 [128], replicated, may hold values from 0.1 to 1.9
- cache_keys: bfloat16 [16, 4096, 1024], P(('groups', 'wide'), 'tp'), parts along dimension 0, may hold values from -6 to 6
- cache_values: bfloat16 [16, 4096, 1024], P(('groups', 'wide'), 'tp'), parts along dimension 0, may hold values from -6 to 6
- queries: bfloat16 [16, 2, 8192], P(('groups', 'wide')), parts along dimension 0, may hold values from -128 to 128
- lengths: int32 [16], P(('groups', 'wide')), parts along dimension 0, may hold values from 2 to 4094, as said below
- owner_map: int32 [16], P('groups'), parts along dimension 0, may hold values from 0 to 7, each once
Outputs:
- new_entries: bfloat16 [16, 2, 2048], P(('groups', 'wide')), parts along dimension 0
- attended: bfloat16 [16, 2, 8192], P(('groups', 'wide')), parts along dimension 0
The draws below stay inside these ranges and needn't reach their ends.
There are 2 independent parts, one for each index of `groups`. The reference program is written for one: setup_inputs(seed, part) draws one part's arguments, and reference() takes and returns one part's arrays. A program takes and returns all parts, laid end to end along the dimension named above; an argument that names none is the same for every part. Nothing has to cross between parts.
Inputs may be any that keep to these rules, and one draw needn't show every extreme that they name: `lengths`: some row has exactly 4094 cached tokens. `owner_map`: each value appears once.
All inputs are finite; a program needn't handle non-finite values.
Results may differ from the reference program's by a relative error of at most 0.0055.
Values may be sent and summed in bfloat16 or wider, within the bound.
A program may use at most 128 MiB of HBM per device.

```python
import jax
import jax.numpy as jnp
from jax import lax

D = 5120
Q_HEADS = 64
KV_HEADS = 8
HEAD = 128
RANK = 64
CACHE = 4096
KVD = 1024
HALF = 2560
BLOCK = 320
SHARDS = 8
ROWS = 8
N_TP = 2


def cache_base(key):
    return jax.random.normal(key, (ROWS, CACHE, KVD), jnp.float32)


def draw_cache_keys(key, part):
    base_normals = cache_base(key)
    return jnp.clip(base_normals, -6.0, 6.0).astype(jnp.bfloat16)


def draw_queries(key, part):
    key = jax.random.fold_in(key, 23)
    query_noise = jax.random.normal(key, (ROWS, 2, Q_HEADS, HEAD), jnp.float32)
    values = 2.0 * query_noise
    return jnp.clip(values, -128.0, 128.0).reshape(ROWS, 2, Q_HEADS * HEAD).astype(jnp.bfloat16)


def draw_lengths(key, part):
    key = jax.random.fold_in(key, 37)
    top_power = CACHE.bit_length() - 1
    power_draw = jax.random.randint(jax.random.fold_in(key, 1), (ROWS,), 1, top_power + 1)
    short_span = jnp.left_shift(jnp.ones((ROWS,), jnp.int32), power_draw.astype(jnp.int32))
    raw_draw = jax.random.randint(jax.random.fold_in(key, 2), (ROWS,), 0, CACHE, dtype=jnp.int32)
    strength_pick = jax.random.randint(jax.random.fold_in(key, 3), (ROWS,), 0, 4)
    short_length = 2 + raw_draw % short_span
    long_length = CACHE // 2 + raw_draw % (CACHE // 2 - 1)
    length = jnp.minimum(jnp.where(strength_pick == 0, short_length, long_length), CACHE - 2)
    chosen = jax.random.randint(jax.random.fold_in(key, 4), (), 0, ROWS)
    length = jnp.where(jnp.arange(ROWS) == chosen, CACHE - 2, length)
    return length.astype(jnp.int32)


def shard_levels(rng, dims, split, least, high):
    level, own = 1.0, jax.random.fold_in(rng, 6)
    for axis_at, shards_of in split:
        draws = jnp.exp(jax.random.uniform(jax.random.fold_in(own, axis_at), (shards_of,), jnp.float32, least / len(split), high / len(split)))
        level = level * jnp.repeat(draws, dims[axis_at] // shards_of).reshape([-1 if axis == axis_at else 1 for axis in range(len(dims))])
    return level


def normal_values(key, dims, spread, most, cuts=(), kind=jnp.bfloat16):
    entries = jax.random.normal(key, dims, jnp.float32) * spread
    if len(cuts) > 0:
        entries = shard_levels(key, dims, cuts, -0.22, 0.18) * entries
    return jnp.clip(entries, min=-most, max=most).astype(kind)


def setup_inputs(seed: int = 0, part: int = 0) -> dict:
    seeds = jax.random.split(jax.random.key(seed), 11)
    own_keys = jax.random.split(jax.random.fold_in(seeds[10], part), 11)
    hidden = normal_values(own_keys[0], (ROWS, 2, D), 1.0, 6.0, ((0, 8),))
    kv_weight = normal_values(seeds[1], (D, 2 * KVD), D ** -0.5, 0.078125, ((0, 2),))
    adapter_down = normal_values(seeds[2], (N_TP, HALF, 2 * RANK), D ** -0.5, 0.078125, ((0, 2), (1, 8)), jnp.float32)
    adapter_up = normal_values(seeds[3], (RANK, 2 * KVD), (4 * RANK) ** -0.5, 0.375, ((1, 16),), jnp.float32)
    key_gain = jnp.clip(1.0 + 0.18 * jax.random.normal(seeds[4], (HEAD,), jnp.float32), 0.1, 1.9)
    cache_keys = draw_cache_keys(jax.random.fold_in(jax.random.fold_in(seeds[10], part), 71), part)
    cache_values = normal_values(own_keys[6], (ROWS, CACHE, KVD), 1.0, 6.0, ((0, 8), (1, 2)))
    queries = draw_queries(jax.random.fold_in(jax.random.fold_in(seeds[10], part), 71), part)
    lengths = draw_lengths(jax.random.fold_in(jax.random.fold_in(seeds[10], part), 71), part)
    owner_map = jax.random.permutation(own_keys[9], SHARDS).astype(jnp.int32)
    return {"hidden": hidden, "kv_weight": kv_weight, "adapter_down": adapter_down, "adapter_up": adapter_up, "key_gain": key_gain, "cache_keys": cache_keys, "cache_values": cache_values, "queries": queries, "lengths": lengths, "owner_map": owner_map}


ADAPTER_SCALE = 2.0
ROPE_BASE = 1000000.0
NORM_EPSILON = 1e-06
FAR_BELOW = -1e+30

def rotate(normed, positions):
    inverse_frequency = ROPE_BASE ** (-(jnp.arange(HEAD // 2, dtype=jnp.float32) * (2.0 / HEAD)))
    angles = positions[:, :, None, None] * inverse_frequency
    cosine = jnp.cos(angles)
    sine_table = jnp.sin(angles)
    lower_half = normed[..., :HEAD // 2]
    upper_half = normed[..., HEAD // 2:]
    return jnp.concatenate([lower_half * cosine - upper_half * sine_table, upper_half * cosine + lower_half * sine_table], axis=-1)

def fresh_entries(summed, key_gain, lengths):
    row_count = summed.shape[0]
    key_heads = summed[..., :KVD].reshape(row_count, 2, KV_HEADS, HEAD)
    value_part = summed[..., KVD:]
    normed = key_heads * lax.rsqrt(lax.optimization_barrier(jnp.mean(key_heads * key_heads, axis=-1, keepdims=True)) + NORM_EPSILON) * key_gain
    positions = (lengths[:, None] + jnp.arange(2, dtype=jnp.int32)[None, :]).astype(jnp.float32)
    new_keys = rotate(normed, positions).reshape(row_count, 2, KVD).astype(jnp.bfloat16)
    return jnp.concatenate([new_keys, value_part.astype(jnp.bfloat16)], axis=-1)

def finish(query_heads, row_entries, cache_max, cache_total, cache_mix):
    new_keys = row_entries[:, :KVD].reshape(2, KV_HEADS, HEAD).astype(jnp.float32)
    new_values = row_entries[:, KVD:].reshape(2, KV_HEADS, HEAD).astype(jnp.float32)
    scores = jnp.einsum('sghd,tgd->sght', query_heads, new_keys) * HEAD ** (-0.5)
    causal = (jnp.arange(2)[:, None] >= jnp.arange(2)[None, :])[:, None, None, :]
    masked = jnp.where(causal, scores, FAR_BELOW)
    row_max = jnp.maximum(cache_max, lax.optimization_barrier(jnp.max(masked, axis=-1)))
    new_weights = jnp.exp(masked - row_max[..., None])
    rescale = jnp.exp(cache_max - row_max)
    rounded = lax.optimization_barrier(new_weights.astype(jnp.bfloat16)).astype(jnp.float32)
    mixed = rescale[..., None] * cache_mix + jnp.einsum('sght,tgd->sghd', rounded, new_values)
    denominator = rescale * cache_total + lax.optimization_barrier(jnp.sum(new_weights, axis=-1))
    return (mixed / denominator[..., None]).reshape(2, Q_HEADS * HEAD).astype(jnp.bfloat16)

def reference(hidden, kv_weight, adapter_down, adapter_up, key_gain, cache_keys, cache_values, queries, lengths, owner_map):
    stored = adapter_down.reshape(N_TP, SHARDS, BLOCK, 2 * RANK)
    ordered = jnp.take(stored, owner_map, axis=1).reshape(D, 2 * RANK)
    adapter_delta = jnp.concatenate([jnp.dot(ordered[:, :RANK], adapter_up[:, :KVD], preferred_element_type=jnp.float32, precision=lax.Precision.HIGHEST), jnp.dot(ordered[:, RANK:], adapter_up[:, KVD:], preferred_element_type=jnp.float32, precision=lax.Precision.HIGHEST)], axis=1)
    merged = (kv_weight.astype(jnp.float32) + ADAPTER_SCALE * adapter_delta).astype(jnp.bfloat16)
    summed = jnp.dot(hidden.reshape(ROWS * 2, D), merged, preferred_element_type=jnp.float32).reshape(ROWS, 2, 2 * KVD)
    new_entries = fresh_entries(summed, key_gain, lengths)
    group = Q_HEADS // KV_HEADS

    def one_row(items):
        row_queries, row_keys, row_values, row_length, row_entries = items
        query_heads = row_queries.reshape(2, KV_HEADS, group, HEAD).astype(jnp.float32)
        key_block = row_keys.reshape(CACHE, KV_HEADS, HEAD).astype(jnp.float32)
        value_block = row_values.reshape(CACHE, KV_HEADS, HEAD).astype(jnp.float32)
        scores = jnp.einsum('sghd,pgd->sghp', query_heads, key_block) * HEAD ** (-0.5)
        valid = jnp.arange(CACHE, dtype=jnp.int32) < row_length
        masked = jnp.where(valid, scores, FAR_BELOW)
        cache_max = lax.optimization_barrier(jnp.max(masked, axis=-1))
        weights = jnp.exp(masked - cache_max[..., None])
        cache_total = lax.optimization_barrier(jnp.sum(weights, axis=-1))
        rounded = lax.optimization_barrier(weights.astype(jnp.bfloat16)).astype(jnp.float32)
        cache_mix = jnp.einsum('sghp,pgd->sghd', rounded, value_block)
        return finish(query_heads, row_entries, cache_max, cache_total, cache_mix)
    attended = lax.map(one_row, (queries, cache_keys, cache_values, lengths, new_entries))
    return (new_entries, attended)
```

```python
import functools

import jax
import jax.numpy as jnp
import numpy as np
from jax import lax
from jax.experimental import pallas as pl
from jax.experimental.pallas import tpu as pltpu
from jax.sharding import PartitionSpec as P

Q_HEADS = 64
KV_HEADS = 8
HEAD = 128
RANK = 64
KVD = 1024

ADAPTER_SCALE = 2.0
ROPE_BASE = 1000000.0
NORM_EPSILON = 1e-06
FAR_BELOW = -1e30
SCORE_SCALE = HEAD ** (-0.5)

LANES = 128
CHUNK = 256
QUERIES = 2 * Q_HEADS
MESH = pl.DeviceIdType.MESH


def window_of(block_rows):
    return -(-block_rows // LANES) * LANES


def kernel(
    n,
    hidden_ref,
    down_ref,
    up_ref,
    gain_ref,
    freq_ref,
    queries_ref,
    lengths_ref,
    owner_ref,
    weight_hbm,
    keys_hbm,
    values_hbm,
    entries_ref,
    attended_ref,
    key_buf,
    value_buf,
    weight_buf,
    scores,
    block_queries,
    query_rows,
    stage_a,
    land_a,
    rows_a,
    rows_b,
    stage_b,
    land_b,
    up_here,
    up_all,
    mine,
    theirs,
    proj_mine,
    proj_theirs,
    key_rows,
    value_rows,
    out_rows,
    key_sem,
    value_sem,
    weight_sem,
    send_a,
    recv_a,
    send_b,
    recv_b,
    send_up,
    recv_up,
    send_x,
    recv_x,
    send_p,
    recv_p,
):
    w = lax.axis_index("wide")
    t = lax.axis_index("tp")
    other = 1 - t
    block_rows = down_ref.shape[1]
    half = weight_hbm.shape[0]
    span = keys_hbm.shape[1]
    key_chunks = span // CHUNK
    weight_chunks = half // CHUNK
    window = window_of(block_rows)

    barrier = pltpu.get_barrier_semaphore()
    for d in range(n):
        peer = lax.rem(w + d, n)
        if d > 0:
            pl.semaphore_signal(
                barrier, inc=1, device_id={"wide": peer, "tp": t}, device_id_type=MESH
            )
        pl.semaphore_signal(
            barrier, inc=1, device_id={"wide": peer, "tp": other}, device_id_type=MESH
        )

    def key_copy(c):
        return pltpu.make_async_copy(
            keys_hbm.at[0, pl.ds(c * CHUNK, CHUNK), :], key_buf.at[c], key_sem.at[c]
        )

    def value_copy(c):
        return pltpu.make_async_copy(
            values_hbm.at[0, pl.ds(c * CHUNK, CHUNK), :], value_buf.at[c], value_sem.at[c]
        )

    def weight_copy(c):
        return pltpu.make_async_copy(
            weight_hbm.at[pl.ds(c * CHUNK, CHUNK), :], weight_buf.at[c], weight_sem.at[c]
        )

    for c in range(key_chunks):
        key_copy(c).start()
    for c in range(key_chunks):
        value_copy(c).start()
    for c in range(weight_chunks):
        weight_copy(c).start()

    owners = [owner_ref[b] for b in range(n)]

    blocks = []
    for b in range(n):
        near = (b * block_rows) // LANES * LANES
        away = b * block_rows - near
        reach = -(-(away + block_rows) // LANES) * LANES
        start = pl.multiple_of(t * half + near, LANES)
        piece = hidden_ref[0, :, pl.ds(start, reach)].astype(jnp.float32)
        piece = piece[:, away : away + block_rows]
        if window > block_rows:
            piece = jnp.concatenate(
                [piece, jnp.zeros((2, window - block_rows), jnp.float32)], axis=1
            )
        blocks.append(piece)
    for d in range(n):
        peer = lax.rem(w + d, n)
        piece = blocks[0]
        for b in range(1, n):
            piece = jnp.where(owners[b] == peer, blocks[b], piece)
        if d == 0:
            land_a[w] = piece
        else:
            stage_a[peer] = piece

    up_here[...] = up_ref[...].astype(jnp.bfloat16)

    pl.semaphore_wait(barrier, 2 * n - 1)

    def a_copy(peer):
        return pltpu.make_async_remote_copy(
            src_ref=stage_a.at[peer],
            dst_ref=land_a.at[w],
            send_sem=send_a.at[peer],
            recv_sem=recv_a.at[w],
            device_id={"wide": peer, "tp": t},
            device_id_type=MESH,
        )

    def a_wait(peer):
        pltpu.make_async_remote_copy(
            src_ref=stage_a.at[peer],
            dst_ref=land_a.at[peer],
            send_sem=send_a.at[peer],
            recv_sem=recv_a.at[peer],
            device_id={"wide": peer, "tp": t},
            device_id_type=MESH,
        ).wait_recv()

    for d in range(1, n):
        a_copy(lax.rem(w + d, n)).start()

    shard = 2 * w + t
    side = lax.div(shard, n)
    slot = lax.rem(shard, n)

    def up_copy(peer):
        return pltpu.make_async_remote_copy(
            src_ref=up_here,
            dst_ref=up_all.at[slot],
            send_sem=send_up.at[peer],
            recv_sem=recv_up.at[slot],
            device_id={"wide": peer, "tp": side},
            device_id_type=MESH,
        )

    for d in range(1, n):
        up_copy(lax.rem(w + d, n)).start()

    @pl.when(side == t)
    def _():
        up_all[slot] = up_here[...]

    @pl.when(side != t)
    def _():
        up_copy(w).start()

    for j in range(Q_HEADS):
        query_rows[2 * j : 2 * j + 2, :] = queries_ref[
            0, :, LANES * j : LANES * (j + 1)
        ].astype(jnp.float32)
    turned = query_rows[...].T
    column_head = lax.shift_right_logical(
        lax.broadcasted_iota(jnp.int32, (HEAD, QUERIES), 1), 4
    )
    for g in range(KV_HEADS):
        block_queries[g * HEAD : (g + 1) * HEAD, :] = jnp.where(
            column_head == g, turned, 0.0
        ).astype(jnp.bfloat16)

    length = lengths_ref[0]
    first = t * span

    def score_step(c, top):
        key_copy(c).wait()
        found = (
            jnp.dot(key_buf[c], block_queries[...], preferred_element_type=jnp.float32)
            * SCORE_SCALE
        )
        position = first + c * CHUNK + lax.broadcasted_iota(jnp.int32, (CHUNK, QUERIES), 0)
        found = jnp.where(position < length, found, FAR_BELOW)
        scores[c] = found
        return jnp.maximum(top, jnp.max(found, axis=0, keepdims=True))

    top = lax.fori_loop(
        0, key_chunks, score_step, jnp.full((1, QUERIES), FAR_BELOW, jnp.float32)
    )

    placed = down_ref[0]
    if window > block_rows:
        placed = jnp.concatenate(
            [placed, jnp.zeros((window - block_rows, 2 * RANK), jnp.float32)], axis=0
        )
    high = placed.astype(jnp.bfloat16)
    low = (placed - high.astype(jnp.float32)).astype(jnp.bfloat16)
    for d in range(1, n):
        a_wait(lax.rem(w + d, n))
    for r in range(n):
        rows_a[2 * r : 2 * r + 2, :] = land_a[r]
    both = jnp.dot(
        rows_a[...].astype(jnp.bfloat16),
        jnp.concatenate([high, low], axis=1),
        preferred_element_type=jnp.float32,
    )
    rows_b[...] = both[:, : 2 * RANK] + both[:, 2 * RANK :]
    for r in range(n):
        stage_b[r] = rows_b[2 * r : 2 * r + 2, :]
    land_b[shard] = stage_b[w]

    def b_copy(peer, side_to):
        return pltpu.make_async_remote_copy(
            src_ref=stage_b.at[peer],
            dst_ref=land_b.at[shard],
            send_sem=send_b.at[2 * peer + side_to],
            recv_sem=recv_b.at[shard],
            device_id={"wide": peer, "tp": side_to},
            device_id_type=MESH,
        )

    def b_wait(peer, side_from):
        pltpu.make_async_remote_copy(
            src_ref=stage_b.at[peer],
            dst_ref=land_b.at[2 * peer + side_from],
            send_sem=send_b.at[2 * peer + side_from],
            recv_sem=recv_b.at[2 * peer + side_from],
            device_id={"wide": peer, "tp": side_from},
            device_id_type=MESH,
        ).wait_recv()

    for d in range(n):
        peer = lax.rem(w + d, n)
        if d > 0:
            b_copy(peer, t).start()
        b_copy(peer, other).start()

    def value_step(c, carry):
        total, mixes = carry
        weights = jnp.exp(scores[c] - top)
        total = total + jnp.sum(weights, axis=0, keepdims=True)
        across = weights.T.astype(jnp.bfloat16)
        value_copy(c).wait()
        added = []
        for p in range(KV_HEADS // 2):
            added.append(
                mixes[p]
                + jnp.dot(
                    across[32 * p : 32 * p + 32, :],
                    value_buf[c, :, 2 * HEAD * p : 2 * HEAD * (p + 1)],
                    preferred_element_type=jnp.float32,
                )
            )
        return total, tuple(added)

    total, mixes = lax.fori_loop(
        0,
        key_chunks,
        value_step,
        (
            jnp.zeros((1, QUERIES), jnp.float32),
            tuple(jnp.zeros((32, 2 * HEAD), jnp.float32) for _ in range(KV_HEADS // 2)),
        ),
    )
    for p in range(KV_HEADS // 2):
        mine[32 * p : 32 * p + 16, :] = mixes[p][:16, :HEAD]
        mine[32 * p + 16 : 32 * p + 32, :] = mixes[p][16:, HEAD:]
    which = lax.broadcasted_iota(jnp.int32, (8, QUERIES), 0)
    mine[QUERIES : QUERIES + 8, :] = jnp.where(which == 0, top, total)
    x_copy = pltpu.make_async_remote_copy(
        src_ref=mine,
        dst_ref=theirs,
        send_sem=send_x,
        recv_sem=recv_x,
        device_id={"wide": w, "tp": other},
        device_id_type=MESH,
    )
    x_copy.start()

    def weight_step(c, carry):
        weight_copy(c).wait()
        start = pl.multiple_of(t * half + c * CHUNK, CHUNK)
        return carry + jnp.dot(
            hidden_ref[0, :, pl.ds(start, CHUNK)],
            weight_buf[c],
            preferred_element_type=jnp.float32,
        )

    proj_mine[...] = lax.fori_loop(
        0, weight_chunks, weight_step, jnp.zeros((2, 2 * KVD), jnp.float32)
    )

    for d in range(n):
        peer = lax.rem(w + d, n)
        if d > 0:
            b_wait(peer, t)
        b_wait(peer, other)
    inner = land_b[0]
    for i in range(1, 2 * n):
        inner = inner + land_b[i]
    inner = jnp.where(t == 0, inner[:, :RANK], inner[:, RANK:]) * ADAPTER_SCALE
    inner_high = inner.astype(jnp.bfloat16)
    inner_low = (inner - inner_high.astype(jnp.float32)).astype(jnp.bfloat16)
    for k in range(n):
        source = t * n + k

        @pl.when(source != shard)
        def _():
            pltpu.make_async_remote_copy(
                src_ref=up_here,
                dst_ref=up_all.at[k],
                send_sem=send_up.at[k],
                recv_sem=recv_up.at[k],
                device_id={"wide": w, "tp": other},
                device_id_type=MESH,
            ).wait_recv()

    up_side = jnp.concatenate([up_all[k] for k in range(n)], axis=1)
    delta = jnp.dot(inner_high, up_side, preferred_element_type=jnp.float32) + jnp.dot(
        inner_low, up_side, preferred_element_type=jnp.float32
    )
    columns = pl.ds(pl.multiple_of(t * KVD, KVD), KVD)
    proj_mine[:, columns] = proj_mine[:, columns] + delta
    p_copy = pltpu.make_async_remote_copy(
        src_ref=proj_mine,
        dst_ref=proj_theirs,
        send_sem=send_p,
        recv_sem=recv_p,
        device_id={"wide": w, "tp": other},
        device_id_type=MESH,
    )
    p_copy.start()

    row_step = lax.broadcasted_iota(jnp.int32, (2 * KV_HEADS, HEAD), 0) & 1
    lane = lax.broadcasted_iota(jnp.int32, (2 * KV_HEADS, HEAD), 1)
    angles = (length + row_step).astype(jnp.float32) * freq_ref[...]
    cosine = jnp.cos(angles)
    sine = jnp.where(lane < HEAD // 2, -jnp.sin(angles), jnp.sin(angles))

    x_copy.wait_recv()
    first_side = t == 0
    lower = jnp.where(first_side, mine[...], theirs[...])
    upper = jnp.where(first_side, theirs[...], mine[...])
    low_top, low_total = lower[QUERIES : QUERIES + 1], lower[QUERIES + 1 : QUERIES + 2]
    up_top, up_total = upper[QUERIES : QUERIES + 1], upper[QUERIES + 1 : QUERIES + 2]
    cache_top = jnp.maximum(low_top, up_top)
    low_factor = jnp.exp(low_top - cache_top)
    up_factor = jnp.exp(up_top - cache_top)
    cache_total = low_factor * low_total + up_factor * up_total

    def as_rows(line):
        return jnp.broadcast_to(line, (QUERIES, QUERIES)).T

    cache_mix = as_rows(low_factor) * lower[:QUERIES] + as_rows(up_factor) * upper[:QUERIES]
    top_rows = as_rows(cache_top)
    total_rows = as_rows(cache_total)

    p_copy.wait_recv()
    summed = proj_mine[...] + proj_theirs[...]
    for g in range(KV_HEADS):
        key_rows[2 * g : 2 * g + 2, :] = summed[:, HEAD * g : HEAD * (g + 1)]
        value_rows[2 * g : 2 * g + 2, :] = summed[:, KVD + HEAD * g : KVD + HEAD * (g + 1)]
    heads = key_rows[...]
    normed = (
        heads
        * lax.rsqrt(jnp.mean(heads * heads, axis=-1, keepdims=True) + NORM_EPSILON)
        * gain_ref[...]
    )
    rotated = normed * cosine + pltpu.roll(normed, HEAD // 2, 1) * sine
    new_keys = rotated.astype(jnp.bfloat16)
    new_values = value_rows[...].astype(jnp.bfloat16)
    key_rows[...] = rotated
    for g in range(KV_HEADS):
        entries_ref[0, :, HEAD * g : HEAD * (g + 1)] = key_rows[2 * g : 2 * g + 2, :].astype(
            jnp.bfloat16
        )
    entries_ref[0, :, KVD:] = summed[:, KVD:].astype(jnp.bfloat16)

    fresh = (
        lax.dot_general(
            query_rows[...].astype(jnp.bfloat16),
            new_keys,
            (((1,), (1,)), ((), ())),
            preferred_element_type=jnp.float32,
        )
        * SCORE_SCALE
    )
    row = lax.broadcasted_iota(jnp.int32, (QUERIES, 2 * KV_HEADS), 0)
    column = lax.broadcasted_iota(jnp.int32, (QUERIES, 2 * KV_HEADS), 1)
    seen = (lax.shift_right_logical(row, 4) == lax.shift_right_logical(column, 1)) & (
        (column & 1) <= (row & 1)
    )
    masked = jnp.where(seen, fresh, FAR_BELOW)
    row_max = jnp.maximum(top_rows[:, :1], jnp.max(masked, axis=-1, keepdims=True))
    new_weights = jnp.exp(masked - row_max)
    rescale = jnp.exp(top_rows - row_max)
    mixed = rescale * cache_mix + jnp.dot(
        new_weights.astype(jnp.bfloat16), new_values, preferred_element_type=jnp.float32
    )
    denominator = rescale * total_rows + jnp.sum(new_weights, axis=-1, keepdims=True)
    out_rows[...] = mixed / denominator
    for j in range(Q_HEADS):
        attended_ref[0, :, LANES * j : LANES * (j + 1)] = out_rows[
            2 * j : 2 * j + 2, :
        ].astype(jnp.bfloat16)

    for d in range(n):
        peer = lax.rem(w + d, n)
        if d > 0:
            a_copy(peer).wait_send()
            up_copy(peer).wait_send()
            b_copy(peer, t).wait_send()
        b_copy(peer, other).wait_send()

    @pl.when(side != t)
    def _():
        up_copy(w).wait_send()

    x_copy.wait_send()
    p_copy.wait_send()


def body(
    hidden,
    kv_weight,
    adapter_down,
    adapter_up,
    key_gain,
    cache_keys,
    cache_values,
    queries,
    lengths,
    owner_map,
):
    n = lax.axis_size("wide")
    half, width = kv_weight.shape
    span = cache_keys.shape[1]
    block_rows = adapter_down.shape[1]
    key_chunks = span // CHUNK
    weight_chunks = half // CHUNK
    window = window_of(block_rows)
    up_columns = adapter_up.shape[1]
    frequency = ROPE_BASE ** (-(np.arange(HEAD // 2, dtype=np.float64) * (2.0 / HEAD)))
    frequency = np.concatenate([frequency, frequency]).astype(np.float32)[None, :]
    f32, bf16 = jnp.float32, jnp.bfloat16
    vmem = pl.BlockSpec(memory_space=pltpu.VMEM)
    smem = pl.BlockSpec(memory_space=pltpu.SMEM)
    hbm = pl.BlockSpec(memory_space=pl.ANY)
    dma = pltpu.SemaphoreType.DMA
    return pl.pallas_call(
        functools.partial(kernel, n),
        out_shape=(
            jax.ShapeDtypeStruct((1, 2, width), bf16),
            jax.ShapeDtypeStruct((1, 2, Q_HEADS * HEAD), bf16),
        ),
        in_specs=[vmem] * 6 + [smem] * 2 + [hbm] * 3,
        out_specs=(vmem, vmem),
        scratch_shapes=[
            pltpu.VMEM((key_chunks, CHUNK, KVD), bf16),
            pltpu.VMEM((key_chunks, CHUNK, KVD), bf16),
            pltpu.VMEM((weight_chunks, CHUNK, width), bf16),
            pltpu.VMEM((key_chunks, CHUNK, QUERIES), f32),
            pltpu.VMEM((KVD, QUERIES), bf16),
            pltpu.VMEM((QUERIES, HEAD), f32),
            pltpu.VMEM((n, 2, window), f32),
            pltpu.VMEM((n, 2, window), f32),
            pltpu.VMEM((2 * n, window), f32),
            pltpu.VMEM((2 * n, 2 * RANK), f32),
            pltpu.VMEM((n, 2, 2 * RANK), f32),
            pltpu.VMEM((2 * n, 2, 2 * RANK), f32),
            pltpu.VMEM((RANK, up_columns), bf16),
            pltpu.VMEM((n, RANK, up_columns), bf16),
            pltpu.VMEM((QUERIES + 8, HEAD), f32),
            pltpu.VMEM((QUERIES + 8, HEAD), f32),
            pltpu.VMEM((2, width), f32),
            pltpu.VMEM((2, width), f32),
            pltpu.VMEM((2 * KV_HEADS, HEAD), f32),
            pltpu.VMEM((2 * KV_HEADS, HEAD), f32),
            pltpu.VMEM((QUERIES, HEAD), f32),
            dma((key_chunks,)),
            dma((key_chunks,)),
            dma((weight_chunks,)),
            dma((n,)),
            dma((n,)),
            dma((2 * n,)),
            dma((2 * n,)),
            dma((n,)),
            dma((n,)),
            dma,
            dma,
            dma,
            dma,
        ],
        compiler_params=pltpu.CompilerParams(
            collective_id=0, has_side_effects=True, vmem_limit_bytes=48 * 1024 * 1024
        ),
    )(
        hidden,
        adapter_down,
        adapter_up,
        key_gain.reshape(1, HEAD),
        jnp.asarray(frequency),
        queries,
        lengths,
        owner_map,
        kv_weight,
        cache_keys,
        cache_values,
    )


def solution(mesh):
    return jax.shard_map(
        body,
        mesh=mesh,
        in_specs=(
            P(("groups", "wide"), None, None),
            P("tp", None),
            P("tp", "wide", None),
            P(None, ("wide", "tp")),
            P(),
            P(("groups", "wide"), "tp", None),
            P(("groups", "wide"), "tp", None),
            P(("groups", "wide"), None, None),
            P(("groups", "wide")),
            P("groups"),
        ),
        out_specs=(P(("groups", "wide"), None, None), P(("groups", "wide"), None, None)),
        check_vma=False,
    )
```

```python
import functools

import jax
import jax.numpy as jnp
import numpy as np
from jax import lax
from jax.experimental import pallas as pl
from jax.experimental.pallas import tpu as pltpu
from jax.sharding import PartitionSpec as P

Q_HEADS = 64
KV_HEADS = 8
HEAD = 128
RANK = 64
KVD = 1024

ADAPTER_SCALE = 2.0
ROPE_BASE = 1000000.0
NORM_EPSILON = 1e-06
FAR_BELOW = -1e30
SCORE_SCALE = HEAD ** (-0.5)

LANES = 128
CHUNK = 256
QUERIES = 2 * Q_HEADS
MESH = pl.DeviceIdType.MESH


def window_of(block_rows):
    return -(-block_rows // LANES) * LANES


def kernel(
    n,
    hidden_hbm,
    down_hbm,
    up_hbm,
    gain_hbm,
    freq_hbm,
    queries_hbm,
    lengths_hbm,
    owner_hbm,
    weight_hbm,
    keys_hbm,
    values_hbm,
    entries_ref,
    attended_ref,
    hidden_ref,
    down_ref,
    up_ref,
    gain_ref,
    freq_ref,
    queries_ref,
    lengths_ref,
    owner_ref,
    small_sem,
    key_buf,
    value_buf,
    weight_buf,
    scores,
    block_queries,
    query_rows,
    stage_a,
    land_a,
    rows_a,
    rows_b,
    stage_b,
    land_b,
    up_here,
    up_all,
    mine,
    theirs,
    proj_mine,
    proj_theirs,
    key_rows,
    value_rows,
    out_rows,
    key_sem,
    value_sem,
    weight_sem,
    send_a,
    recv_a,
    send_b,
    recv_b,
    send_up,
    recv_up,
    send_x,
    recv_x,
    send_p,
    recv_p,
):
    w = lax.axis_index("wide")
    t = lax.axis_index("tp")
    other = 1 - t
    block_rows = down_hbm.shape[1]
    half = weight_hbm.shape[0]
    span = keys_hbm.shape[1]
    key_chunks = span // CHUNK
    weight_chunks = half // CHUNK
    window = window_of(block_rows)

    small = [
        pltpu.make_async_copy(source, target, small_sem.at[i])
        for i, (source, target) in enumerate(
            (
                (owner_hbm, owner_ref),
                (hidden_hbm, hidden_ref),
                (up_hbm, up_ref),
                (queries_hbm, queries_ref),
                (lengths_hbm, lengths_ref),
                (down_hbm, down_ref),
                (gain_hbm, gain_ref),
                (freq_hbm, freq_ref),
            )
        )
    ]
    for copy in small:
        copy.start()

    barrier = pltpu.get_barrier_semaphore()
    for d in range(n):
        peer = lax.rem(w + d, n)
        if d > 0:
            pl.semaphore_signal(
                barrier, inc=1, device_id={"wide": peer, "tp": t}, device_id_type=MESH
            )
        pl.semaphore_signal(
            barrier, inc=1, device_id={"wide": peer, "tp": other}, device_id_type=MESH
        )

    def key_copy(c):
        return pltpu.make_async_copy(
            keys_hbm.at[0, pl.ds(c * CHUNK, CHUNK), :], key_buf.at[c], key_sem.at[c]
        )

    def value_copy(c):
        return pltpu.make_async_copy(
            values_hbm.at[0, pl.ds(c * CHUNK, CHUNK), :], value_buf.at[c], value_sem.at[c]
        )

    def weight_copy(c):
        return pltpu.make_async_copy(
            weight_hbm.at[pl.ds(c * CHUNK, CHUNK), :], weight_buf.at[c], weight_sem.at[c]
        )

    for c in range(key_chunks):
        key_copy(c).start()
    for c in range(key_chunks):
        value_copy(c).start()
    for c in range(weight_chunks):
        weight_copy(c).start()

    for copy in small[:3]:
        copy.wait()

    owners = [owner_ref[b] for b in range(n)]

    blocks = []
    for b in range(n):
        near = (b * block_rows) // LANES * LANES
        away = b * block_rows - near
        reach = -(-(away + block_rows) // LANES) * LANES
        start = pl.multiple_of(t * half + near, LANES)
        piece = hidden_ref[0, :, pl.ds(start, reach)].astype(jnp.float32)
        piece = piece[:, away : away + block_rows]
        if window > block_rows:
            piece = jnp.concatenate(
                [piece, jnp.zeros((2, window - block_rows), jnp.float32)], axis=1
            )
        blocks.append(piece)
    for d in range(n):
        peer = lax.rem(w + d, n)
        piece = blocks[0]
        for b in range(1, n):
            piece = jnp.where(owners[b] == peer, blocks[b], piece)
        if d == 0:
            land_a[w] = piece
        else:
            stage_a[peer] = piece

    up_here[...] = up_ref[...].astype(jnp.bfloat16)

    pl.semaphore_wait(barrier, 2 * n - 1)

    def a_copy(peer):
        return pltpu.make_async_remote_copy(
            src_ref=stage_a.at[peer],
            dst_ref=land_a.at[w],
            send_sem=send_a.at[peer],
            recv_sem=recv_a.at[w],
            device_id={"wide": peer, "tp": t},
            device_id_type=MESH,
        )

    def a_wait(peer):
        pltpu.make_async_remote_copy(
            src_ref=stage_a.at[peer],
            dst_ref=land_a.at[peer],
            send_sem=send_a.at[peer],
            recv_sem=recv_a.at[peer],
            device_id={"wide": peer, "tp": t},
            device_id_type=MESH,
        ).wait_recv()

    for d in range(1, n):
        a_copy(lax.rem(w + d, n)).start()

    shard = 2 * w + t
    side = lax.div(shard, n)
    slot = lax.rem(shard, n)

    def up_copy(peer):
        return pltpu.make_async_remote_copy(
            src_ref=up_here,
            dst_ref=up_all.at[slot],
            send_sem=send_up.at[peer],
            recv_sem=recv_up.at[slot],
            device_id={"wide": peer, "tp": side},
            device_id_type=MESH,
        )

    for d in range(1, n):
        up_copy(lax.rem(w + d, n)).start()

    @pl.when(side == t)
    def _():
        up_all[slot] = up_here[...]

    @pl.when(side != t)
    def _():
        up_copy(w).start()

    for copy in small[3:]:
        copy.wait()

    for j in range(Q_HEADS):
        query_rows[2 * j : 2 * j + 2, :] = queries_ref[
            0, :, LANES * j : LANES * (j + 1)
        ].astype(jnp.float32)
    turned = query_rows[...].T
    column_head = lax.shift_right_logical(
        lax.broadcasted_iota(jnp.int32, (HEAD, QUERIES), 1), 4
    )
    for g in range(KV_HEADS):
        block_queries[g * HEAD : (g + 1) * HEAD, :] = jnp.where(
            column_head == g, turned, 0.0
        ).astype(jnp.bfloat16)

    length = lengths_ref[0]
    first = t * span

    def score_step(c, top):
        key_copy(c).wait()
        found = (
            jnp.dot(key_buf[c], block_queries[...], preferred_element_type=jnp.float32)
            * SCORE_SCALE
        )
        position = first + c * CHUNK + lax.broadcasted_iota(jnp.int32, (CHUNK, QUERIES), 0)
        found = jnp.where(position < length, found, FAR_BELOW)
        scores[c] = found
        return jnp.maximum(top, jnp.max(found, axis=0, keepdims=True))

    top = lax.fori_loop(
        0, key_chunks, score_step, jnp.full((1, QUERIES), FAR_BELOW, jnp.float32)
    )

    placed = down_ref[0]
    if window > block_rows:
        placed = jnp.concatenate(
            [placed, jnp.zeros((window - block_rows, 2 * RANK), jnp.float32)], axis=0
        )
    high = placed.astype(jnp.bfloat16)
    low = (placed - high.astype(jnp.float32)).astype(jnp.bfloat16)
    for d in range(1, n):
        a_wait(lax.rem(w + d, n))
    for r in range(n):
        rows_a[2 * r : 2 * r + 2, :] = land_a[r]
    both = jnp.dot(
        rows_a[...].astype(jnp.bfloat16),
        jnp.concatenate([high, low], axis=1),
        preferred_element_type=jnp.float32,
    )
    rows_b[...] = both[:, : 2 * RANK] + both[:, 2 * RANK :]
    for r in range(n):
        stage_b[r] = rows_b[2 * r : 2 * r + 2, :]
    land_b[shard] = stage_b[w]

    def b_copy(peer, side_to):
        return pltpu.make_async_remote_copy(
            src_ref=stage_b.at[peer],
            dst_ref=land_b.at[shard],
            send_sem=send_b.at[2 * peer + side_to],
            recv_sem=recv_b.at[shard],
            device_id={"wide": peer, "tp": side_to},
            device_id_type=MESH,
        )

    def b_wait(peer, side_from):
        pltpu.make_async_remote_copy(
            src_ref=stage_b.at[peer],
            dst_ref=land_b.at[2 * peer + side_from],
            send_sem=send_b.at[2 * peer + side_from],
            recv_sem=recv_b.at[2 * peer + side_from],
            device_id={"wide": peer, "tp": side_from},
            device_id_type=MESH,
        ).wait_recv()

    for d in range(n):
        peer = lax.rem(w + d, n)
        if d > 0:
            b_copy(peer, t).start()
        b_copy(peer, other).start()

    def value_step(c, carry):
        total, mixes = carry
        weights = jnp.exp(scores[c] - top)
        total = total + jnp.sum(weights, axis=0, keepdims=True)
        across = weights.T.astype(jnp.bfloat16)
        value_copy(c).wait()
        added = []
        for p in range(KV_HEADS // 2):
            added.append(
                mixes[p]
                + jnp.dot(
                    across[32 * p : 32 * p + 32, :],
                    value_buf[c, :, 2 * HEAD * p : 2 * HEAD * (p + 1)],
                    preferred_element_type=jnp.float32,
                )
            )
        return total, tuple(added)

    total, mixes = lax.fori_loop(
        0,
        key_chunks,
        value_step,
        (
            jnp.zeros((1, QUERIES), jnp.float32),
            tuple(jnp.zeros((32, 2 * HEAD), jnp.float32) for _ in range(KV_HEADS // 2)),
        ),
    )
    for p in range(KV_HEADS // 2):
        mine[32 * p : 32 * p + 16, :] = mixes[p][:16, :HEAD]
        mine[32 * p + 16 : 32 * p + 32, :] = mixes[p][16:, HEAD:]
    which = lax.broadcasted_iota(jnp.int32, (8, QUERIES), 0)
    mine[QUERIES : QUERIES + 8, :] = jnp.where(which == 0, top, total)
    x_copy = pltpu.make_async_remote_copy(
        src_ref=mine,
        dst_ref=theirs,
        send_sem=send_x,
        recv_sem=recv_x,
        device_id={"wide": w, "tp": other},
        device_id_type=MESH,
    )
    x_copy.start()

    def weight_step(c, carry):
        weight_copy(c).wait()
        start = pl.multiple_of(t * half + c * CHUNK, CHUNK)
        return carry + jnp.dot(
            hidden_ref[0, :, pl.ds(start, CHUNK)],
            weight_buf[c],
            preferred_element_type=jnp.float32,
        )

    proj_mine[...] = lax.fori_loop(
        0, weight_chunks, weight_step, jnp.zeros((2, 2 * KVD), jnp.float32)
    )

    for d in range(n):
        peer = lax.rem(w + d, n)
        if d > 0:
            b_wait(peer, t)
        b_wait(peer, other)
    inner = land_b[0]
    for i in range(1, 2 * n):
        inner = inner + land_b[i]
    inner = jnp.where(t == 0, inner[:, :RANK], inner[:, RANK:]) * ADAPTER_SCALE
    inner_high = inner.astype(jnp.bfloat16)
    inner_low = (inner - inner_high.astype(jnp.float32)).astype(jnp.bfloat16)
    for k in range(n):
        source = t * n + k

        @pl.when(source != shard)
        def _():
            pltpu.make_async_remote_copy(
                src_ref=up_here,
                dst_ref=up_all.at[k],
                send_sem=send_up.at[k],
                recv_sem=recv_up.at[k],
                device_id={"wide": w, "tp": other},
                device_id_type=MESH,
            ).wait_recv()

    up_side = jnp.concatenate([up_all[k] for k in range(n)], axis=1)
    delta = jnp.dot(inner_high, up_side, preferred_element_type=jnp.float32) + jnp.dot(
        inner_low, up_side, preferred_element_type=jnp.float32
    )
    columns = pl.ds(pl.multiple_of(t * KVD, KVD), KVD)
    proj_mine[:, columns] = proj_mine[:, columns] + delta
    p_copy = pltpu.make_async_remote_copy(
        src_ref=proj_mine,
        dst_ref=proj_theirs,
        send_sem=send_p,
        recv_sem=recv_p,
        device_id={"wide": w, "tp": other},
        device_id_type=MESH,
    )
    p_copy.start()

    row_step = lax.broadcasted_iota(jnp.int32, (2 * KV_HEADS, HEAD), 0) & 1
    lane = lax.broadcasted_iota(jnp.int32, (2 * KV_HEADS, HEAD), 1)
    angles = (length + row_step).astype(jnp.float32) * freq_ref[...]
    cosine = jnp.cos(angles)
    sine = jnp.where(lane < HEAD // 2, -jnp.sin(angles), jnp.sin(angles))

    x_copy.wait_recv()
    first_side = t == 0
    lower = jnp.where(first_side, mine[...], theirs[...])
    upper = jnp.where(first_side, theirs[...], mine[...])
    low_top, low_total = lower[QUERIES : QUERIES + 1], lower[QUERIES + 1 : QUERIES + 2]
    up_top, up_total = upper[QUERIES : QUERIES + 1], upper[QUERIES + 1 : QUERIES + 2]
    cache_top = jnp.maximum(low_top, up_top)
    low_factor = jnp.exp(low_top - cache_top)
    up_factor = jnp.exp(up_top - cache_top)
    cache_total = low_factor * low_total + up_factor * up_total

    def as_rows(line):
        return jnp.broadcast_to(line, (QUERIES, QUERIES)).T

    cache_mix = as_rows(low_factor) * lower[:QUERIES] + as_rows(up_factor) * upper[:QUERIES]
    top_rows = as_rows(cache_top)
    total_rows = as_rows(cache_total)

    p_copy.wait_recv()
    summed = proj_mine[...] + proj_theirs[...]
    for g in range(KV_HEADS):
        key_rows[2 * g : 2 * g + 2, :] = summed[:, HEAD * g : HEAD * (g + 1)]
        value_rows[2 * g : 2 * g + 2, :] = summed[:, KVD + HEAD * g : KVD + HEAD * (g + 1)]
    heads = key_rows[...]
    normed = (
        heads
        * lax.rsqrt(jnp.mean(heads * heads, axis=-1, keepdims=True) + NORM_EPSILON)
        * gain_ref[...]
    )
    rotated = normed * cosine + pltpu.roll(normed, HEAD // 2, 1) * sine
    new_keys = rotated.astype(jnp.bfloat16)
    new_values = value_rows[...].astype(jnp.bfloat16)
    key_rows[...] = rotated
    for g in range(KV_HEADS):
        entries_ref[0, :, HEAD * g : HEAD * (g + 1)] = key_rows[2 * g : 2 * g + 2, :].astype(
            jnp.bfloat16
        )
    entries_ref[0, :, KVD:] = summed[:, KVD:].astype(jnp.bfloat16)

    fresh = (
        lax.dot_general(
            query_rows[...].astype(jnp.bfloat16),
            new_keys,
            (((1,), (1,)), ((), ())),
            preferred_element_type=jnp.float32,
        )
        * SCORE_SCALE
    )
    row = lax.broadcasted_iota(jnp.int32, (QUERIES, 2 * KV_HEADS), 0)
    column = lax.broadcasted_iota(jnp.int32, (QUERIES, 2 * KV_HEADS), 1)
    seen = (lax.shift_right_logical(row, 4) == lax.shift_right_logical(column, 1)) & (
        (column & 1) <= (row & 1)
    )
    masked = jnp.where(seen, fresh, FAR_BELOW)
    row_max = jnp.maximum(top_rows[:, :1], jnp.max(masked, axis=-1, keepdims=True))
    new_weights = jnp.exp(masked - row_max)
    rescale = jnp.exp(top_rows - row_max)
    mixed = rescale * cache_mix + jnp.dot(
        new_weights.astype(jnp.bfloat16), new_values, preferred_element_type=jnp.float32
    )
    denominator = rescale * total_rows + jnp.sum(new_weights, axis=-1, keepdims=True)
    out_rows[...] = mixed / denominator
    for j in range(Q_HEADS):
        attended_ref[0, :, LANES * j : LANES * (j + 1)] = out_rows[
            2 * j : 2 * j + 2, :
        ].astype(jnp.bfloat16)

    for d in range(n):
        peer = lax.rem(w + d, n)
        if d > 0:
            a_copy(peer).wait_send()
            up_copy(peer).wait_send()
            b_copy(peer, t).wait_send()
        b_copy(peer, other).wait_send()

    @pl.when(side != t)
    def _():
        up_copy(w).wait_send()

    x_copy.wait_send()
    p_copy.wait_send()


def body(
    hidden,
    kv_weight,
    adapter_down,
    adapter_up,
    key_gain,
    cache_keys,
    cache_values,
    queries,
    lengths,
    owner_map,
):
    n = lax.axis_size("wide")
    half, width = kv_weight.shape
    span = cache_keys.shape[1]
    block_rows = adapter_down.shape[1]
    key_chunks = span // CHUNK
    weight_chunks = half // CHUNK
    window = window_of(block_rows)
    up_columns = adapter_up.shape[1]
    frequency = ROPE_BASE ** (-(np.arange(HEAD // 2, dtype=np.float64) * (2.0 / HEAD)))
    frequency = np.concatenate([frequency, frequency]).astype(np.float32)[None, :]
    f32, bf16 = jnp.float32, jnp.bfloat16
    vmem = pl.BlockSpec(memory_space=pltpu.VMEM)
    hbm = pl.BlockSpec(memory_space=pltpu.HBM)
    dma = pltpu.SemaphoreType.DMA
    return pl.pallas_call(
        functools.partial(kernel, n),
        out_shape=(
            jax.ShapeDtypeStruct((1, 2, width), bf16),
            jax.ShapeDtypeStruct((1, 2, Q_HEADS * HEAD), bf16),
        ),
        in_specs=[hbm] * 11,
        out_specs=(vmem, vmem),
        scratch_shapes=[
            pltpu.VMEM(hidden.shape, bf16),
            pltpu.VMEM(adapter_down.shape, f32),
            pltpu.VMEM(adapter_up.shape, f32),
            pltpu.VMEM((1, HEAD), f32),
            pltpu.VMEM((1, HEAD), f32),
            pltpu.VMEM(queries.shape, bf16),
            pltpu.SMEM(lengths.shape, jnp.int32),
            pltpu.SMEM(owner_map.shape, jnp.int32),
            dma((8,)),
            pltpu.VMEM((key_chunks, CHUNK, KVD), bf16),
            pltpu.VMEM((key_chunks, CHUNK, KVD), bf16),
            pltpu.VMEM((weight_chunks, CHUNK, width), bf16),
            pltpu.VMEM((key_chunks, CHUNK, QUERIES), f32),
            pltpu.VMEM((KVD, QUERIES), bf16),
            pltpu.VMEM((QUERIES, HEAD), f32),
            pltpu.VMEM((n, 2, window), f32),
            pltpu.VMEM((n, 2, window), f32),
            pltpu.VMEM((2 * n, window), f32),
            pltpu.VMEM((2 * n, 2 * RANK), f32),
            pltpu.VMEM((n, 2, 2 * RANK), f32),
            pltpu.VMEM((2 * n, 2, 2 * RANK), f32),
            pltpu.VMEM((RANK, up_columns), bf16),
            pltpu.VMEM((n, RANK, up_columns), bf16),
            pltpu.VMEM((QUERIES + 8, HEAD), f32),
            pltpu.VMEM((QUERIES + 8, HEAD), f32),
            pltpu.VMEM((2, width), f32),
            pltpu.VMEM((2, width), f32),
            pltpu.VMEM((2 * KV_HEADS, HEAD), f32),
            pltpu.VMEM((2 * KV_HEADS, HEAD), f32),
            pltpu.VMEM((QUERIES, HEAD), f32),
            dma((key_chunks,)),
            dma((key_chunks,)),
            dma((weight_chunks,)),
            dma((n,)),
            dma((n,)),
            dma((2 * n,)),
            dma((2 * n,)),
            dma((n,)),
            dma((n,)),
            dma,
            dma,
            dma,
            dma,
        ],
        compiler_params=pltpu.CompilerParams(
            collective_id=0, has_side_effects=True, vmem_limit_bytes=62 * 1024 * 1024
        ),
    )(
        hidden,
        adapter_down,
        adapter_up,
        key_gain.reshape(1, HEAD),
        jnp.asarray(frequency),
        queries,
        lengths,
        owner_map,
        kv_weight,
        cache_keys,
        cache_values,
    )


def solution(mesh):
    return jax.shard_map(
        body,
        mesh=mesh,
        in_specs=(
            P(("groups", "wide"), None, None),
            P("tp", None),
            P("tp", "wide", None),
            P(None, ("wide", "tp")),
            P(),
            P(("groups", "wide"), "tp", None),
            P(("groups", "wide"), "tp", None),
            P(("groups", "wide"), None, None),
            P(("groups", "wide")),
            P("groups"),
        ),
        out_specs=(P(("groups", "wide"), None, None), P(("groups", "wide"), None, None)),
        check_vma=False,
    )
```

```python
import functools

import jax
import jax.numpy as jnp
import numpy as np
from jax import lax
from jax.experimental import pallas as pl
from jax.experimental.pallas import tpu as pltpu
from jax.sharding import PartitionSpec as P

Q_HEADS = 64
KV_HEADS = 8
HEAD = 128
RANK = 64
KVD = 1024

ADAPTER_SCALE = 2.0
ROPE_BASE = 1000000.0
NORM_EPSILON = 1e-06
FAR_BELOW = -1e30
SCORE_SCALE = HEAD ** (-0.5)

LANES = 128
CHUNK = 256
QUERIES = 2 * Q_HEADS
MESH = pl.DeviceIdType.MESH


def window_of(block_rows):
    return -(-block_rows // LANES) * LANES


def kernel(
    n,
    hidden_hbm,
    down_hbm,
    up_hbm,
    gain_hbm,
    freq_hbm,
    queries_hbm,
    lengths_hbm,
    owner_hbm,
    weight_hbm,
    keys_hbm,
    values_hbm,
    entries_ref,
    attended_ref,
    hidden_ref,
    down_ref,
    up_ref,
    gain_ref,
    freq_ref,
    queries_ref,
    lengths_ref,
    owner_ref,
    small_sem,
    key_buf,
    value_buf,
    weight_buf,
    scores,
    block_queries,
    query_rows,
    stage_a,
    land_a,
    rows_a,
    rows_b,
    stage_b,
    land_b,
    up_here,
    up_all,
    mine,
    theirs,
    proj_mine,
    proj_theirs,
    key_rows,
    value_rows,
    out_rows,
    key_sem,
    value_sem,
    weight_sem,
    send_a,
    recv_a,
    send_b,
    recv_b,
    send_up,
    recv_up,
    send_x,
    recv_x,
    send_p,
    recv_p,
):
    w = lax.axis_index("wide")
    t = lax.axis_index("tp")
    other = 1 - t
    block_rows = down_hbm.shape[1]
    half = weight_hbm.shape[0]
    span = keys_hbm.shape[1]
    key_chunks = span // CHUNK
    weight_chunks = half // CHUNK
    window = window_of(block_rows)

    small = [
        pltpu.make_async_copy(source, target, small_sem.at[i])
        for i, (source, target) in enumerate(
            (
                (owner_hbm, owner_ref),
                (hidden_hbm, hidden_ref),
                (up_hbm, up_ref),
                (queries_hbm, queries_ref),
                (lengths_hbm, lengths_ref),
                (down_hbm, down_ref),
                (gain_hbm, gain_ref),
                (freq_hbm, freq_ref),
            )
        )
    ]
    for copy in small:
        copy.start()

    barrier = pltpu.get_barrier_semaphore()
    for d in range(n):
        peer = lax.rem(w + d, n)
        if d > 0:
            pl.semaphore_signal(
                barrier, inc=1, device_id={"wide": peer, "tp": t}, device_id_type=MESH
            )
        pl.semaphore_signal(
            barrier, inc=1, device_id={"wide": peer, "tp": other}, device_id_type=MESH
        )

    def key_copy(c):
        return pltpu.make_async_copy(
            keys_hbm.at[0, pl.ds(c * CHUNK, CHUNK), :], key_buf.at[c], key_sem.at[c]
        )

    def value_copy(c):
        return pltpu.make_async_copy(
            values_hbm.at[0, pl.ds(c * CHUNK, CHUNK), :], value_buf.at[c], value_sem.at[c]
        )

    def weight_copy(c):
        return pltpu.make_async_copy(
            weight_hbm.at[pl.ds(c * CHUNK, CHUNK), :], weight_buf.at[c], weight_sem.at[c]
        )

    for c in range(key_chunks):
        key_copy(c).start()
    for c in range(key_chunks):
        value_copy(c).start()
    for c in range(weight_chunks):
        weight_copy(c).start()

    for copy in small[:3]:
        copy.wait()

    owners = [owner_ref[b] for b in range(n)]

    blocks = []
    for b in range(n):
        near = (b * block_rows) // LANES * LANES
        away = b * block_rows - near
        reach = -(-(away + block_rows) // LANES) * LANES
        start = pl.multiple_of(t * half + near, LANES)
        piece = hidden_ref[0, :, pl.ds(start, reach)].astype(jnp.float32)
        piece = piece[:, away : away + block_rows]
        if window > block_rows:
            piece = jnp.concatenate(
                [piece, jnp.zeros((2, window - block_rows), jnp.float32)], axis=1
            )
        blocks.append(piece)
    for d in range(n):
        peer = lax.rem(w + d, n)
        piece = blocks[0]
        for b in range(1, n):
            piece = jnp.where(owners[b] == peer, blocks[b], piece)
        if d == 0:
            land_a[w] = piece
        else:
            stage_a[peer] = piece

    up_here[...] = up_ref[...].astype(jnp.bfloat16)

    pl.semaphore_wait(barrier, 2 * n - 1)

    def a_copy(peer):
        return pltpu.make_async_remote_copy(
            src_ref=stage_a.at[peer],
            dst_ref=land_a.at[w],
            send_sem=send_a.at[peer],
            recv_sem=recv_a.at[w],
            device_id={"wide": peer, "tp": t},
            device_id_type=MESH,
        )

    def a_wait(peer):
        pltpu.make_async_remote_copy(
            src_ref=stage_a.at[peer],
            dst_ref=land_a.at[peer],
            send_sem=send_a.at[peer],
            recv_sem=recv_a.at[peer],
            device_id={"wide": peer, "tp": t},
            device_id_type=MESH,
        ).wait_recv()

    for d in range(1, n):
        a_copy(lax.rem(w + d, n)).start()

    shard = 2 * w + t
    side = lax.div(shard, n)
    slot = lax.rem(shard, n)

    def up_copy(peer):
        return pltpu.make_async_remote_copy(
            src_ref=up_here,
            dst_ref=up_all.at[slot],
            send_sem=send_up.at[peer],
            recv_sem=recv_up.at[slot],
            device_id={"wide": peer, "tp": side},
            device_id_type=MESH,
        )

    for d in range(1, n):
        up_copy(lax.rem(w + d, n)).start()

    @pl.when(side == t)
    def _():
        up_all[slot] = up_here[...]

    @pl.when(side != t)
    def _():
        up_copy(w).start()

    for copy in small[3:]:
        copy.wait()

    for j in range(Q_HEADS):
        query_rows[2 * j : 2 * j + 2, :] = queries_ref[
            0, :, LANES * j : LANES * (j + 1)
        ].astype(jnp.float32)
    turned = query_rows[...].T
    column_head = lax.shift_right_logical(
        lax.broadcasted_iota(jnp.int32, (HEAD, QUERIES), 1), 4
    )
    for g in range(KV_HEADS):
        block_queries[g * HEAD : (g + 1) * HEAD, :] = jnp.where(
            column_head == g, turned, 0.0
        ).astype(jnp.bfloat16)

    length = lengths_ref[0]
    first = t * span

    def score_step(c, top):
        key_copy(c).wait()
        found = (
            jnp.dot(key_buf[c], block_queries[...], preferred_element_type=jnp.float32)
            * SCORE_SCALE
        )
        position = first + c * CHUNK + lax.broadcasted_iota(jnp.int32, (CHUNK, QUERIES), 0)
        found = jnp.where(position < length, found, FAR_BELOW)
        scores[c] = found
        return jnp.maximum(top, jnp.max(found, axis=0, keepdims=True))

    top = lax.fori_loop(
        0, key_chunks, score_step, jnp.full((1, QUERIES), FAR_BELOW, jnp.float32)
    )

    placed = down_ref[0]
    if window > block_rows:
        placed = jnp.concatenate(
            [placed, jnp.zeros((window - block_rows, 2 * RANK), jnp.float32)], axis=0
        )
    high = placed.astype(jnp.bfloat16)
    low = (placed - high.astype(jnp.float32)).astype(jnp.bfloat16)
    for d in range(1, n):
        a_wait(lax.rem(w + d, n))
    for r in range(n):
        rows_a[2 * r : 2 * r + 2, :] = land_a[r]
    both = jnp.dot(
        rows_a[...].astype(jnp.bfloat16),
        jnp.concatenate([high, low], axis=1),
        preferred_element_type=jnp.float32,
    )
    rows_b[...] = both[:, : 2 * RANK] + both[:, 2 * RANK :]
    for r in range(n):
        stage_b[r] = rows_b[2 * r : 2 * r + 2, :]
    land_b[shard] = stage_b[w]

    def b_copy(peer, side_to):
        return pltpu.make_async_remote_copy(
            src_ref=stage_b.at[peer],
            dst_ref=land_b.at[shard],
            send_sem=send_b.at[2 * peer + side_to],
            recv_sem=recv_b.at[shard],
            device_id={"wide": peer, "tp": side_to},
            device_id_type=MESH,
        )

    def b_wait(peer, side_from):
        pltpu.make_async_remote_copy(
            src_ref=stage_b.at[peer],
            dst_ref=land_b.at[2 * peer + side_from],
            send_sem=send_b.at[2 * peer + side_from],
            recv_sem=recv_b.at[2 * peer + side_from],
            device_id={"wide": peer, "tp": side_from},
            device_id_type=MESH,
        ).wait_recv()

    for d in range(n):
        peer = lax.rem(w + d, n)
        if d > 0:
            b_copy(peer, t).start()
        b_copy(peer, other).start()

    def value_step(c, carry):
        total, mixes = carry
        weights = jnp.exp(scores[c] - top)
        total = total + jnp.sum(weights, axis=0, keepdims=True)
        across = weights.T.astype(jnp.bfloat16)
        value_copy(c).wait()
        added = []
        for p in range(KV_HEADS // 2):
            added.append(
                mixes[p]
                + jnp.dot(
                    across[32 * p : 32 * p + 32, :],
                    value_buf[c, :, 2 * HEAD * p : 2 * HEAD * (p + 1)],
                    preferred_element_type=jnp.float32,
                )
            )
        return total, tuple(added)

    total, mixes = lax.fori_loop(
        0,
        key_chunks,
        value_step,
        (
            jnp.zeros((1, QUERIES), jnp.float32),
            tuple(jnp.zeros((32, 2 * HEAD), jnp.float32) for _ in range(KV_HEADS // 2)),
        ),
    )
    for p in range(KV_HEADS // 2):
        mine[32 * p : 32 * p + 16, :] = mixes[p][:16, :HEAD]
        mine[32 * p + 16 : 32 * p + 32, :] = mixes[p][16:, HEAD:]
    which = lax.broadcasted_iota(jnp.int32, (8, QUERIES), 0)
    mine[QUERIES : QUERIES + 8, :] = jnp.where(which == 0, top, total)
    x_copy = pltpu.make_async_remote_copy(
        src_ref=mine,
        dst_ref=theirs,
        send_sem=send_x,
        recv_sem=recv_x,
        device_id={"wide": w, "tp": other},
        device_id_type=MESH,
    )
    x_copy.start()

    def weight_step(c, carry):
        weight_copy(c).wait()
        start = pl.multiple_of(t * half + c * CHUNK, CHUNK)
        return carry + jnp.dot(
            hidden_ref[0, :, pl.ds(start, CHUNK)],
            weight_buf[c],
            preferred_element_type=jnp.float32,
        )

    proj_mine[...] = lax.fori_loop(
        0, weight_chunks, weight_step, jnp.zeros((2, 2 * KVD), jnp.float32)
    )

    for d in range(n):
        peer = lax.rem(w + d, n)
        if d > 0:
            b_wait(peer, t)
        b_wait(peer, other)
    inner = land_b[0]
    for i in range(1, 2 * n):
        inner = inner + land_b[i]
    inner = jnp.where(t == 0, inner[:, :RANK], inner[:, RANK:]) * ADAPTER_SCALE
    inner_high = inner.astype(jnp.bfloat16)
    inner_low = (inner - inner_high.astype(jnp.float32)).astype(jnp.bfloat16)
    for k in range(n):
        source = t * n + k

        @pl.when(source != shard)
        def _():
            pltpu.make_async_remote_copy(
                src_ref=up_here,
                dst_ref=up_all.at[k],
                send_sem=send_up.at[k],
                recv_sem=recv_up.at[k],
                device_id={"wide": w, "tp": other},
                device_id_type=MESH,
            ).wait_recv()

    up_side = jnp.concatenate([up_all[k] for k in range(n)], axis=1)
    delta = jnp.dot(inner_high, up_side, preferred_element_type=jnp.float32) + jnp.dot(
        inner_low, up_side, preferred_element_type=jnp.float32
    )
    columns = pl.ds(pl.multiple_of(t * KVD, KVD), KVD)
    proj_mine[:, columns] = proj_mine[:, columns] + delta
    p_copy = pltpu.make_async_remote_copy(
        src_ref=proj_mine,
        dst_ref=proj_theirs,
        send_sem=send_p,
        recv_sem=recv_p,
        device_id={"wide": w, "tp": other},
        device_id_type=MESH,
    )
    p_copy.start()

    row_step = lax.broadcasted_iota(jnp.int32, (2 * KV_HEADS, HEAD), 0) & 1
    lane = lax.broadcasted_iota(jnp.int32, (2 * KV_HEADS, HEAD), 1)
    angles = (length + row_step).astype(jnp.float32) * freq_ref[...]
    cosine = jnp.cos(angles)
    sine = jnp.where(lane < HEAD // 2, -jnp.sin(angles), jnp.sin(angles))

    x_copy.wait_recv()
    first_side = t == 0
    lower = jnp.where(first_side, mine[...], theirs[...])
    upper = jnp.where(first_side, theirs[...], mine[...])
    low_top, low_total = lower[QUERIES : QUERIES + 1], lower[QUERIES + 1 : QUERIES + 2]
    up_top, up_total = upper[QUERIES : QUERIES + 1], upper[QUERIES + 1 : QUERIES + 2]
    cache_top = jnp.maximum(low_top, up_top)
    low_factor = jnp.exp(low_top - cache_top)
    up_factor = jnp.exp(up_top - cache_top)
    cache_total = low_factor * low_total + up_factor * up_total

    def as_rows(line):
        return jnp.broadcast_to(line, (QUERIES, QUERIES)).T

    cache_mix = as_rows(low_factor) * lower[:QUERIES] + as_rows(up_factor) * upper[:QUERIES]
    top_rows = as_rows(cache_top)
    total_rows = as_rows(cache_total)

    p_copy.wait_recv()
    summed = proj_mine[...] + proj_theirs[...]
    for g in range(KV_HEADS):
        key_rows[2 * g : 2 * g + 2, :] = summed[:, HEAD * g : HEAD * (g + 1)]
        value_rows[2 * g : 2 * g + 2, :] = summed[:, KVD + HEAD * g : KVD + HEAD * (g + 1)]
    heads = key_rows[...]
    normed = (
        heads
        * lax.rsqrt(jnp.mean(heads * heads, axis=-1, keepdims=True) + NORM_EPSILON)
        * gain_ref[...]
    )
    rotated = normed * cosine + pltpu.roll(normed, HEAD // 2, 1) * sine
    new_keys = rotated.astype(jnp.bfloat16)
    new_values = value_rows[...].astype(jnp.bfloat16)
    key_rows[...] = rotated
    for g in range(KV_HEADS):
        entries_ref[0, :, HEAD * g : HEAD * (g + 1)] = key_rows[2 * g : 2 * g + 2, :].astype(
            jnp.bfloat16
        )
    entries_ref[0, :, KVD:] = summed[:, KVD:].astype(jnp.bfloat16)

    fresh = (
        lax.dot_general(
            query_rows[...].astype(jnp.bfloat16),
            new_keys,
            (((1,), (1,)), ((), ())),
            preferred_element_type=jnp.float32,
        )
        * SCORE_SCALE
    )
    row = lax.broadcasted_iota(jnp.int32, (QUERIES, 2 * KV_HEADS), 0)
    column = lax.broadcasted_iota(jnp.int32, (QUERIES, 2 * KV_HEADS), 1)
    seen = (lax.shift_right_logical(row, 4) == lax.shift_right_logical(column, 1)) & (
        (column & 1) <= (row & 1)
    )
    masked = jnp.where(seen, fresh, FAR_BELOW)
    row_max = jnp.maximum(top_rows[:, :1], jnp.max(masked, axis=-1, keepdims=True))
    new_weights = jnp.exp(masked - row_max)
    rescale = jnp.exp(top_rows - row_max)
    mixed = rescale * cache_mix + jnp.dot(
        new_weights.astype(jnp.bfloat16), new_values, preferred_element_type=jnp.float32
    )
    denominator = rescale * total_rows + jnp.sum(new_weights, axis=-1, keepdims=True)
    out_rows[...] = mixed / denominator
    for j in range(Q_HEADS):
        attended_ref[0, :, LANES * j : LANES * (j + 1)] = out_rows[
            2 * j : 2 * j + 2, :
        ].astype(jnp.bfloat16)

    for d in range(n):
        peer = lax.rem(w + d, n)
        if d > 0:
            a_copy(peer).wait_send()
            up_copy(peer).wait_send()
            b_copy(peer, t).wait_send()
        b_copy(peer, other).wait_send()

    @pl.when(side != t)
    def _():
        up_copy(w).wait_send()

    x_copy.wait_send()
    p_copy.wait_send()


def hand_over(entries_in, attended_in, entries_out, attended_out, entries_sem, attended_sem):
    entries_copy = pltpu.make_async_copy(entries_in, entries_out, entries_sem)
    attended_copy = pltpu.make_async_copy(attended_in, attended_out, attended_sem)
    entries_copy.start()
    attended_copy.start()
    entries_copy.wait()
    attended_copy.wait()


def body(
    hidden,
    kv_weight,
    adapter_down,
    adapter_up,
    key_gain,
    cache_keys,
    cache_values,
    queries,
    lengths,
    owner_map,
):
    n = lax.axis_size("wide")
    half, width = kv_weight.shape
    span = cache_keys.shape[1]
    block_rows = adapter_down.shape[1]
    key_chunks = span // CHUNK
    weight_chunks = half // CHUNK
    window = window_of(block_rows)
    up_columns = adapter_up.shape[1]
    frequency = ROPE_BASE ** (-(np.arange(HEAD // 2, dtype=np.float64) * (2.0 / HEAD)))
    frequency = np.concatenate([frequency, frequency]).astype(np.float32)[None, :]
    f32, bf16 = jnp.float32, jnp.bfloat16
    vmem = pl.BlockSpec(memory_space=pltpu.VMEM)
    hbm = pl.BlockSpec(memory_space=pltpu.HBM)
    dma = pltpu.SemaphoreType.DMA
    results = pl.pallas_call(
        functools.partial(kernel, n),
        out_shape=(
            jax.ShapeDtypeStruct((1, 2, width), bf16),
            jax.ShapeDtypeStruct((1, 2, Q_HEADS * HEAD), bf16),
        ),
        in_specs=[hbm] * 11,
        out_specs=(vmem, vmem),
        scratch_shapes=[
            pltpu.VMEM(hidden.shape, bf16),
            pltpu.VMEM(adapter_down.shape, f32),
            pltpu.VMEM(adapter_up.shape, f32),
            pltpu.VMEM((1, HEAD), f32),
            pltpu.VMEM((1, HEAD), f32),
            pltpu.VMEM(queries.shape, bf16),
            pltpu.SMEM(lengths.shape, jnp.int32),
            pltpu.SMEM(owner_map.shape, jnp.int32),
            dma((8,)),
            pltpu.VMEM((key_chunks, CHUNK, KVD), bf16),
            pltpu.VMEM((key_chunks, CHUNK, KVD), bf16),
            pltpu.VMEM((weight_chunks, CHUNK, width), bf16),
            pltpu.VMEM((key_chunks, CHUNK, QUERIES), f32),
            pltpu.VMEM((KVD, QUERIES), bf16),
            pltpu.VMEM((QUERIES, HEAD), f32),
            pltpu.VMEM((n, 2, window), f32),
            pltpu.VMEM((n, 2, window), f32),
            pltpu.VMEM((2 * n, window), f32),
            pltpu.VMEM((2 * n, 2 * RANK), f32),
            pltpu.VMEM((n, 2, 2 * RANK), f32),
            pltpu.VMEM((2 * n, 2, 2 * RANK), f32),
            pltpu.VMEM((RANK, up_columns), bf16),
            pltpu.VMEM((n, RANK, up_columns), bf16),
            pltpu.VMEM((QUERIES + 8, HEAD), f32),
            pltpu.VMEM((QUERIES + 8, HEAD), f32),
            pltpu.VMEM((2, width), f32),
            pltpu.VMEM((2, width), f32),
            pltpu.VMEM((2 * KV_HEADS, HEAD), f32),
            pltpu.VMEM((2 * KV_HEADS, HEAD), f32),
            pltpu.VMEM((QUERIES, HEAD), f32),
            dma((key_chunks,)),
            dma((key_chunks,)),
            dma((weight_chunks,)),
            dma((n,)),
            dma((n,)),
            dma((2 * n,)),
            dma((2 * n,)),
            dma((n,)),
            dma((n,)),
            dma,
            dma,
            dma,
            dma,
        ],
        compiler_params=pltpu.CompilerParams(
            collective_id=0, has_side_effects=True, vmem_limit_bytes=62 * 1024 * 1024
        ),
    )(
        hidden,
        adapter_down,
        adapter_up,
        key_gain.reshape(1, HEAD),
        jnp.asarray(frequency),
        queries,
        lengths,
        owner_map,
        kv_weight,
        cache_keys,
        cache_values,
    )
    return pl.pallas_call(
        hand_over,
        out_shape=tuple(jax.ShapeDtypeStruct(r.shape, r.dtype) for r in results),
        in_specs=[vmem, vmem],
        out_specs=(hbm, hbm),
        scratch_shapes=[dma, dma],
    )(*results)


def solution(mesh):
    return jax.shard_map(
        body,
        mesh=mesh,
        in_specs=(
            P(("groups", "wide"), None, None),
            P("tp", None),
            P("tp", "wide", None),
            P(None, ("wide", "tp")),
            P(),
            P(("groups", "wide"), "tp", None),
            P(("groups", "wide"), "tp", None),
            P(("groups", "wide"), None, None),
            P(("groups", "wide")),
            P("groups"),
        ),
        out_specs=(P(("groups", "wide"), None, None), P(("groups", "wide"), None, None)),
        check_vma=False,
    )
```
